1024 devices in a mesh: tbl: 64 (over y, x), rep: 16 (over z, core).
Axes of the slice: x: 8, y: 8, z: 8, core: 2. Of those that a mesh axis runs over, the one named last changes fastest.
Arguments:
- x_zero: bfloat16 [4096, 24576], P('rep', 'tbl'), may hold values from -6 to 6
- grad_top: bfloat16 [4096, 24576], P('rep', 'tbl'), may hold values from -0.5 to 0.5
- low_zero: bfloat16 [4096, 512], P('rep'), may hold values from -6 to 6
- low_one: bfloat16 [4096, 512], P('rep'), may hold values from -6 to 6
- lift_zero: bfloat16 [512, 24576], P(None, 'tbl'), may hold values from -0.25 to 0.25
- lift_one: bfloat16 [512, 24576], P(None, 'tbl'), may hold values from -0.25 to 0.25
- squeeze_zero: bfloat16 [24576, 512], P('tbl'), may hold values from -0.0390625 to 0.0390625
- squeeze_one: bfloat16 [24576, 512], P('tbl'), may hold values from -0.0390625 to 0.0390625
- bias_zero: float32 [24576], P('tbl'), may hold values from -3 to 3
- bias_one: float32 [24576], P('tbl'), may hold values from -3 to 3
- table_owner: int32 [384], replicated, may hold values from 0 to 63, as said below
- table_slot: int32 [384], replicated, may hold values from 0 to 17
- incidence: int32 [1152, 4096, 128], P('tbl', 'rep'), may hold values 0 or 1
- table_rows: float32 [1152, 8192], P('tbl'), may hold values from -1.5 to 1.5
- row_accum: float32 [1152, 128], P('tbl'), may hold values from 0.1 to 4
Outputs:
- new_rows: float32 [1152, 8192], P('tbl')
- new_accum: float32 [1152, 128], P('tbl')
The draws below stay inside these ranges and needn't reach their ends.
Inputs may be any that keep to these rules, and one draw needn't show every extreme that they name: `table_owner`: no two tables have the same owner and slot; an owner's tables fill its slots from 0 upward; every owner holds 2 or 18 tables, the larger count on a quarter of the owners; an owner holds at most 1 of the tables t with the same t // 6, and some owner holds exactly that many.
All inputs are finite; a program needn't handle non-finite values. No bound on the sum of `incidence` on one device may be relied on, other than what follows from the above.
Results may differ from the reference program's by a relative error of at most 0.0035.
Values may be sent and summed in bfloat16 or wider, within the bound.
No kernel may reach another device: no remote copies, remote signals or barrier semaphores. Data moves between devices by JAX's collectives and lax.ppermute only.
A program may use at most 32 MiB of HBM per device.

```python
import math
import jax
import jax.numpy as jnp
from jax import lax

FEATS = 384
EMB = 64
RANK = 512
ROWS = 256
TOUCH = 128
WIDTH = 24576
SLOT_MAX = 18
SLOTS = 1152
BATCH = 4096
N_TBL = 64
N_REP = 16


def assign_tables(key):
    devices = N_TBL
    per_device = FEATS // N_TBL
    ranking = jax.random.permutation(key, devices)
    counts = jnp.where(ranking < devices // 4, 3 * per_device, per_device // 3).astype(jnp.int32)
    starts = (jnp.cumsum(counts) - counts).astype(jnp.int32)
    tables = jnp.arange(FEATS, dtype=jnp.int32)
    position = tables % per_device * devices + tables // per_device
    owner = (jnp.sum((starts[None, :] <= position[:, None]).astype(jnp.int32), axis=1) - 1).astype(jnp.int32)
    slot = (position - jnp.take(starts, owner)).astype(jnp.int32)
    return (owner, slot)


def draw_table_owner(key, part):
    owner, slot = assign_tables(key)
    return owner


def draw_table_slot(key, part):
    owner, slot = assign_tables(key)
    return slot


def with_ends(entries, stream_key, least, high):
    longest = entries.shape.index(max(entries.shape))
    spots = []
    for shift in (0, 1):
        where = [jax.random.randint(jax.random.fold_in(stream_key, axis), (), 0, length) for axis, length in enumerate(entries.shape)]
        where[longest] = (where[longest] + shift) % entries.shape[longest]
        spots.append(tuple(where))
    return entries.at[spots[0]].set(least).at[spots[1]].set(high)


def steps_of(stream_key, shape, split, least, high):
    gain = 1.0
    for dim, blocks in split:
        heights = jax.random.uniform(jax.random.fold_in(jax.random.fold_in(stream_key, 6), dim), (blocks,), jnp.float32, least / len(split), high / len(split))
        gain = gain * jnp.repeat(jnp.exp(heights), shape[dim] // blocks).reshape((-1,) + (1,) * (len(shape) - 1 - dim))
    return gain


def gaussian(key, shape, deviation, reach, pieces=(), kind=jnp.bfloat16):
    entries = jax.random.normal(key, shape, jnp.float32) * deviation
    if len(pieces) > 0:
        entries = steps_of(key, shape, pieces, -0.22, 0.18) * entries
    return jnp.clip(entries, min=-reach, max=reach).astype(kind)


def setup_inputs(seed: int = 0) -> dict:
    splits = jax.random.split(jax.random.key(seed), 16)
    x_zero = gaussian(splits[0], (BATCH, WIDTH), 1.0, 6.0, ((0, 16), (1, 64)))
    grad_top = gaussian(splits[1], (BATCH, WIDTH), 0.0625, 0.5, ((0, 16), (1, 64)))
    low_zero = gaussian(splits[2], (BATCH, RANK), 1.0, 6.0, ((0, 16),))
    low_one = gaussian(splits[3], (BATCH, RANK), 1.0, 6.0, ((0, 16),))
    lift_zero = gaussian(splits[4], (RANK, WIDTH), RANK ** -0.5, 0.25, ((1, 64),))
    lift_one = gaussian(splits[5], (RANK, WIDTH), RANK ** -0.5, 0.25, ((1, 64),))
    squeeze_zero = gaussian(splits[6], (WIDTH, RANK), WIDTH ** -0.5, 0.0390625, ((0, 64),))
    squeeze_one = gaussian(splits[7], (WIDTH, RANK), WIDTH ** -0.5, 0.0390625, ((0, 64),))
    bias_zero = gaussian(splits[8], (WIDTH,), 0.5, 3.0, ((0, 64),), jnp.float32)
    bias_one = gaussian(splits[9], (WIDTH,), 0.5, 3.0, ((0, 64),), jnp.float32)
    table_owner = draw_table_owner(jax.random.fold_in(splits[15], 71), 0)
    table_slot = draw_table_slot(jax.random.fold_in(splits[15], 71), 0)
    incidence = with_ends((jax.random.randint(splits[12], (SLOTS, BATCH, TOUCH), 0, 16) < 1).astype(jnp.int32), jax.random.fold_in(splits[12], 1), 0, 1)
    table_rows = gaussian(splits[13], (SLOTS, TOUCH * EMB), 0.25, 1.5, ((0, 64),), jnp.float32)
    row_accum = jnp.clip(jnp.exp(math.log(4.0) - 3.6888794 * jax.random.uniform(splits[14], (SLOTS, TOUCH), jnp.float32) ** steps_of(splits[14], (SLOTS, TOUCH), ((0, 64),), -0.2, 0.2)), 0.1, 4.0)
    return dict(x_zero=x_zero, grad_top=grad_top, low_zero=low_zero, low_one=low_one, lift_zero=lift_zero, lift_one=lift_one, squeeze_zero=squeeze_zero, squeeze_one=squeeze_one, bias_zero=bias_zero, bias_one=bias_one, table_owner=table_owner, table_slot=table_slot, incidence=incidence, table_rows=table_rows, row_accum=row_accum)


LEARN_RATE = 0.25
EPSILON = 1e-06

def adagrad(gradient, current, history):
    history_new = history + lax.optimization_barrier(jnp.mean(gradient * gradient, axis=2))
    current_new = current - LEARN_RATE * gradient / (jnp.sqrt(history_new)[:, :, None] + EPSILON)
    return (current_new, history_new)

def reference(x_zero, grad_top, low_zero, low_one, lift_zero, lift_one, squeeze_zero, squeeze_one, bias_zero, bias_one, table_owner, table_slot, incidence, table_rows, row_accum):

    def group(blocks):
        x_block, top_block, zero_block, one_block = blocks
        upstream = top_block.astype(jnp.float32)
        embedded = x_block.astype(jnp.float32)
        gate_one = jnp.dot(one_block, lift_one, preferred_element_type=jnp.float32) + bias_one
        gate_zero = jnp.dot(zero_block, lift_zero, preferred_element_type=jnp.float32) + bias_zero
        rank_one = jnp.dot((upstream * embedded).astype(jnp.bfloat16), lift_one.T, preferred_element_type=jnp.float32).astype(jnp.bfloat16)
        grad_mid = upstream + jnp.dot(rank_one, squeeze_one.T, preferred_element_type=jnp.float32)
        rank_zero = jnp.dot((grad_mid * embedded).astype(jnp.bfloat16), lift_zero.T, preferred_element_type=jnp.float32).astype(jnp.bfloat16)
        pooled_block = upstream * gate_one + grad_mid * gate_zero + grad_mid + jnp.dot(rank_zero, squeeze_zero.T, preferred_element_type=jnp.float32)
        return pooled_block.astype(jnp.bfloat16)
    pooled = lax.map(group, (x_zero.reshape(N_REP, ROWS, WIDTH), grad_top.reshape(N_REP, ROWS, WIDTH), low_zero.reshape(N_REP, ROWS, RANK), low_one.reshape(N_REP, ROWS, RANK)))
    pooled = pooled.reshape(BATCH, FEATS, EMB)
    slot_count = SLOT_MAX
    wanted = jnp.arange(N_TBL * slot_count, dtype=jnp.int32)
    placed = (table_owner * slot_count + table_slot).astype(jnp.int32)
    matches = placed[None, :] == wanted[:, None]
    table_of = lax.optimization_barrier(jnp.sum(jnp.where(matches, jnp.arange(FEATS, dtype=jnp.int32)[None, :], 0), axis=1)).astype(jnp.int32)
    occupied = jnp.any(matches, axis=1)

    def owner_block(owner_index):
        first = (owner_index * slot_count).astype(jnp.int32)
        ids = lax.dynamic_slice_in_dim(table_of, first, slot_count)
        filled = lax.dynamic_slice_in_dim(occupied, first, slot_count)
        columns = jnp.take(pooled, ids, axis=1).astype(jnp.float32) * filled.astype(jnp.float32)[None, :, None]
        incident = lax.dynamic_slice_in_dim(incidence, first, slot_count, 0).astype(jnp.float32)
        return jnp.einsum('sbu,bse->sue', incident, columns)
    row_grads = lax.map(owner_block, jnp.arange(N_TBL, dtype=jnp.int32)).reshape(SLOTS, TOUCH, EMB)
    current_new, history_new = adagrad(row_grads, table_rows.reshape(SLOTS, TOUCH, EMB), row_accum)
    return (current_new.reshape(SLOTS, TOUCH * EMB), history_new)
```

```python
import jax
import jax.numpy as jnp
from jax import lax
from jax.sharding import Mesh, PartitionSpec as P

FEATS = 384
EMB = 64
RANK = 512
ROWS = 256
TOUCH = 128
SLOT_MAX = 18
SLOT_PAD = 24
N_TBL = 64
N_REP = 16
PER_DEV = FEATS // N_TBL

LEARN_RATE = 0.25
EPSILON = 1e-06

TBL = ("y", "x")
REP = ("z", "core")
BF16 = jnp.bfloat16
F32 = jnp.float32


def exchange(blocks, axis):
    return lax.all_to_all(blocks, axis, split_axis=0, concat_axis=0, tiled=True)


def to_tiles(matrix):
    return matrix.reshape(16, 16, 4, 128).transpose(0, 2, 1, 3).reshape(64, 16, 128)


def from_tiles(tiles):
    return tiles.reshape(16, 4, 16, 128).transpose(0, 2, 1, 3).reshape(ROWS, RANK)


def shards(
    x_zero,
    grad_top,
    low_zero,
    low_one,
    lift_zero,
    lift_one,
    squeeze_zero,
    squeeze_one,
    bias_zero,
    bias_one,
    table_owner,
    table_slot,
    incidence,
    table_rows,
    row_accum,
):
    me = lax.axis_index(TBL)
    rep = lax.axis_index(REP)
    core = lax.axis_index("core")
    upstream = grad_top.astype(F32)
    embedded = x_zero.astype(F32)

    tile_rows, tile_cols = rep // 4, rep % 4
    tiles = lax.dynamic_slice(
        squeeze_zero.reshape(PER_DEV, EMB, RANK), (0, tile_rows * 16, tile_cols * 128), (PER_DEV, 16, 128)
    )
    my_owner = lax.dynamic_slice(table_owner, (me * PER_DEV,), (PER_DEV,))
    chosen = (my_owner[None, :] == jnp.arange(N_TBL)[:, None]).astype(BF16)
    squeeze_send = jnp.einsum("ot,trl->orl", chosen, tiles, preferred_element_type=F32).astype(BF16)

    part_one = lax.dot_general(
        (upstream * embedded).astype(BF16), lift_one, (((1,), (1,)), ((), ())), preferred_element_type=F32
    ).astype(BF16)
    got = exchange(jnp.concatenate([to_tiles(part_one), squeeze_send], axis=1), TBL)
    rank_tile = jnp.sum(got[:, :16].astype(F32), axis=0).astype(BF16)
    rank_one = from_tiles(exchange(jnp.broadcast_to(rank_tile[None], (N_TBL, 16, 128)), TBL))

    from_me = (table_owner == me)[None, :] & (table_slot[None, :] == jnp.arange(SLOT_MAX)[:, None])
    source = jnp.any(from_me.reshape(SLOT_MAX, N_TBL, PER_DEV), axis=2).astype(BF16)
    squeeze_slots = jnp.einsum("si,irl->srl", source, got[:, 16:], preferred_element_type=F32).astype(BF16)
    squeeze_all = lax.all_gather(squeeze_slots.reshape(SLOT_MAX * 16, 128), REP, axis=0, tiled=True)
    squeeze_own = (
        squeeze_all.reshape(4, 4, SLOT_MAX, 16, 128).transpose(2, 0, 3, 1, 4).reshape(SLOT_MAX * EMB, RANK)
    )

    gate_one = jnp.dot(low_one, lift_one, preferred_element_type=F32) + bias_one
    gate_zero = jnp.dot(low_zero, lift_zero, preferred_element_type=F32) + bias_zero
    grad_mid = upstream + lax.dot_general(
        rank_one, squeeze_one, (((1,), (1,)), ((), ())), preferred_element_type=F32
    )
    part_zero = lax.dot_general(
        (grad_mid * embedded).astype(BF16), lift_zero, (((1,), (1,)), ((), ())), preferred_element_type=F32
    ).astype(BF16)
    pooled_local = (upstream * gate_one + grad_mid * gate_zero + grad_mid).astype(BF16)
    by_column = pooled_local.reshape(2, 128, PER_DEV, EMB).transpose(3, 0, 2, 1)
    by_column = jnp.pad(by_column, ((0, 0), (0, 0), (0, 8 - PER_DEV), (0, 0))).reshape(N_TBL, 16, 128)
    got = exchange(jnp.concatenate([to_tiles(part_zero), by_column], axis=1), TBL)
    rank_tile = jnp.sum(got[:, :16].astype(F32), axis=0).astype(BF16)

    place = jnp.pad(
        (table_owner * SLOT_PAD + table_slot).reshape(N_TBL, PER_DEV), ((0, 0), (0, 8 - PER_DEV)), constant_values=-1
    ).reshape(-1)
    wanted = (jnp.arange(N_TBL * SLOT_PAD)[:, None] == place[None, :]).astype(BF16)
    halves = got[:, 16:].reshape(N_TBL, 2, 8, 128).transpose(1, 0, 2, 3).reshape(2, N_TBL * 8, 128)
    placed = jnp.einsum("qk,hkb->qhb", wanted, halves, preferred_element_type=F32).astype(BF16)
    placed = placed.reshape(N_TBL, SLOT_PAD, 2, 128).transpose(0, 2, 1, 3).reshape(N_TBL, 2 * SLOT_PAD, 128)
    got = exchange(
        jnp.concatenate([placed, jnp.broadcast_to(rank_tile[None], (N_TBL, 16, 128))], axis=1), TBL
    )
    rank_zero = from_tiles(got[:, 2 * SLOT_PAD :])
    pooled_slots = (
        got[:, : 2 * SLOT_PAD].reshape(EMB, 2, SLOT_PAD, 128)[:, :, :SLOT_MAX].transpose(2, 0, 1, 3)
    ).reshape(SLOT_MAX * EMB, ROWS)
    pooled = (
        pooled_slots.astype(F32)
        + lax.dot_general(squeeze_own, rank_zero, (((1,), (1,)), ((), ())), preferred_element_type=F32)
    ).astype(BF16)
    partial = jnp.einsum(
        "sbu,seb->sue", incidence.astype(BF16), pooled.reshape(SLOT_MAX, EMB, ROWS), preferred_element_type=F32
    )

    half = SLOT_MAX // 2
    partial = partial.reshape(2, half, 8, 8, 128)
    mine = lax.dynamic_index_in_dim(partial, core, 0, keepdims=False)
    theirs = lax.dynamic_index_in_dim(partial, 1 - core, 0, keepdims=False).astype(BF16)
    swap = [(0, 1), (1, 0)]
    paired = (mine + lax.ppermute(theirs, "core", swap).astype(F32)).astype(BF16)
    got = exchange(paired.transpose(1, 0, 2, 3).reshape(8, half * 8, 128), "z")
    summed = jnp.sum(got.astype(F32), axis=0).astype(BF16)
    got = exchange(jnp.broadcast_to(summed[None], (8, half * 8, 128)), "z")
    here = got.reshape(8, half, 8, 128).transpose(1, 0, 2, 3)
    there = lax.ppermute(here, "core", swap)
    gradient = jnp.where(core == 0, jnp.stack([here, there]), jnp.stack([there, here])).astype(F32)
    gradient = gradient.reshape(SLOT_MAX, TOUCH, EMB)
    history_new = row_accum + jnp.mean(gradient * gradient, axis=2)
    rows_new = table_rows.reshape(SLOT_MAX, TOUCH, EMB) - LEARN_RATE * gradient / (
        jnp.sqrt(history_new)[:, :, None] + EPSILON
    )
    return (rows_new.reshape(SLOT_MAX, TOUCH * EMB), history_new)


def solution(mesh):
    grid = Mesh(mesh.devices.reshape(8, 8, 8, 2), TBL + REP)
    in_specs = (
        P(REP, TBL),
        P(REP, TBL),
        P(REP, None),
        P(REP, None),
        P(None, TBL),
        P(None, TBL),
        P(TBL, None),
        P(TBL, None),
        P(TBL),
        P(TBL),
        P(),
        P(),
        P(TBL, REP, None),
        P(TBL, None),
        P(TBL, None),
    )
    out_specs = (P(TBL, None), P(TBL, None))
    return jax.shard_map(shards, mesh=grid, in_specs=in_specs, out_specs=out_specs, check_vma=False)
```

```python
import jax
import jax.numpy as jnp
from jax import lax
from jax.sharding import Mesh, PartitionSpec as P

FEATS = 384
EMB = 64
RANK = 512
ROWS = 256
TOUCH = 128
SLOT_MAX = 18
N_TBL = 64
N_REP = 16
PER_DEV = FEATS // N_TBL

LEARN_RATE = 0.25
EPSILON = 1e-06

TBL = ("y", "x")
REP = ("z", "core")
BF16 = jnp.bfloat16
F32 = jnp.float32


def exchange(blocks, axis):
    return lax.all_to_all(blocks, axis, split_axis=0, concat_axis=0, tiled=True)


def to_tiles(matrix):
    return matrix.reshape(16, 16, 4, 128).transpose(0, 2, 1, 3).reshape(64, 16, 128)


def from_tiles(tiles):
    return tiles.reshape(16, 4, 16, 128).transpose(0, 2, 1, 3).reshape(ROWS, RANK)


def shards(
    x_zero,
    grad_top,
    low_zero,
    low_one,
    lift_zero,
    lift_one,
    squeeze_zero,
    squeeze_one,
    bias_zero,
    bias_one,
    table_owner,
    table_slot,
    incidence,
    table_rows,
    row_accum,
):
    rep = lax.axis_index(REP)
    core = lax.axis_index("core")
    odd = lax.axis_index("z") % 2
    upstream = grad_top.astype(F32)
    embedded = x_zero.astype(F32)

    place = table_owner * SLOT_MAX + table_slot
    wanted = (jnp.arange(N_TBL * SLOT_MAX)[:, None] == place[None, :]).astype(BF16)

    part_one = lax.dot_general(
        (upstream * embedded).astype(BF16), lift_one, (((1,), (1,)), ((), ())), preferred_element_type=F32
    ).astype(BF16)
    quarter = lax.dynamic_slice(squeeze_zero, (0, (2 * odd + core) * 128), (PER_DEV * EMB, 128))
    quarter = quarter.reshape(PER_DEV, EMB, 128).transpose(1, 0, 2)
    got = exchange(jnp.concatenate([to_tiles(part_one), quarter], axis=1), TBL)
    rank_tile = jnp.sum(got[:, :16].astype(F32), axis=0).astype(BF16)
    quarter = jnp.dot(wanted, got[:, 16:].reshape(FEATS, 128), preferred_element_type=F32).astype(BF16)
    got = exchange(
        jnp.concatenate(
            [jnp.broadcast_to(rank_tile[None], (N_TBL, 16, 128)), quarter.reshape(N_TBL, SLOT_MAX, 128)], axis=1
        ),
        TBL,
    )
    rank_one = from_tiles(got[:, :16])

    quarter = got[:, 16:].transpose(1, 0, 2)
    other = lax.ppermute(quarter, "core", [(0, 1), (1, 0)])
    part = jnp.where(core == 0, jnp.concatenate([quarter, other], axis=2), jnp.concatenate([other, quarter], axis=2))
    other = lax.ppermute(part, "z", [(i, i ^ 1) for i in range(8)])
    squeeze_own = jnp.where(odd == 0, jnp.concatenate([part, other], axis=2), jnp.concatenate([other, part], axis=2))

    gate_one = jnp.dot(low_one, lift_one, preferred_element_type=F32) + bias_one
    gate_zero = jnp.dot(low_zero, lift_zero, preferred_element_type=F32) + bias_zero
    grad_mid = upstream + lax.dot_general(
        rank_one, squeeze_one, (((1,), (1,)), ((), ())), preferred_element_type=F32
    )
    part_zero = lax.dot_general(
        (grad_mid * embedded).astype(BF16), lift_zero, (((1,), (1,)), ((), ())), preferred_element_type=F32
    ).astype(BF16)
    pooled_local = (upstream * gate_one + grad_mid * gate_zero + grad_mid).astype(BF16)
    by_column = pooled_local.reshape(2, 128, PER_DEV, EMB).transpose(3, 0, 2, 1).reshape(N_TBL, 2 * PER_DEV, 128)
    got = exchange(jnp.concatenate([to_tiles(part_zero), by_column], axis=1), TBL)
    rank_tile = jnp.sum(got[:, :16].astype(F32), axis=0).astype(BF16)

    placed = [
        jnp.dot(
            wanted,
            got[:, 16 + h * PER_DEV : 16 + (h + 1) * PER_DEV].reshape(FEATS, 128),
            preferred_element_type=F32,
        )
        .astype(BF16)
        .reshape(N_TBL, SLOT_MAX, 128)
        for h in range(2)
    ]
    got = exchange(jnp.concatenate([jnp.broadcast_to(rank_tile[None], (N_TBL, 16, 128))] + placed, axis=1), TBL)
    rank_zero = from_tiles(got[:, :16])
    pooled_slots = (
        got[:, 16:].reshape(EMB, 2, SLOT_MAX, 128).transpose(2, 0, 1, 3).reshape(SLOT_MAX * EMB, ROWS)
    )
    pooled = (
        pooled_slots.astype(F32)
        + lax.dot_general(
            squeeze_own.reshape(SLOT_MAX * EMB, RANK),
            rank_zero,
            (((1,), (1,)), ((), ())),
            preferred_element_type=F32,
        )
    ).astype(BF16)
    partial = jnp.einsum(
        "sbu,seb->sue", incidence.astype(BF16), pooled.reshape(SLOT_MAX, EMB, ROWS), preferred_element_type=F32
    ).astype(BF16)

    share = TOUCH // N_REP
    got = exchange(partial.reshape(SLOT_MAX, N_REP, 4, 128).transpose(1, 0, 2, 3).reshape(N_REP, SLOT_MAX * 4, 128), REP)
    gradient = jnp.sum(got.astype(F32), axis=0).reshape(SLOT_MAX, 4, 2, EMB)
    history = lax.dynamic_slice(row_accum, (0, rep * share), (SLOT_MAX, share)).reshape(SLOT_MAX, 4, 2)
    history_new = history + jnp.mean(gradient * gradient, axis=3)
    update = LEARN_RATE * gradient / (jnp.sqrt(history_new)[:, :, :, None] + EPSILON)
    update = update.astype(BF16).reshape(SLOT_MAX * 4, 128)
    terms, rest = [], history_new.reshape(SLOT_MAX * share)
    for _ in range(3):
        term = lax.reduce_precision(rest, 8, 7)
        terms.append(term)
        rest = rest - term
    terms = jnp.pad(jnp.concatenate(terms).astype(BF16), (0, 8 * 128 - 3 * SLOT_MAX * share)).reshape(8, 128)
    send = jnp.concatenate([update, terms], axis=0)
    got = exchange(jnp.broadcast_to(send[None], (N_REP,) + send.shape), REP)
    update = got[:, : SLOT_MAX * 4].reshape(N_REP, SLOT_MAX, 4 * 128).transpose(1, 0, 2).reshape(SLOT_MAX, TOUCH * EMB)
    terms = got[:, SLOT_MAX * 4 :].reshape(N_REP, 8 * 128)[:, : 3 * SLOT_MAX * share].astype(F32)
    terms = terms.reshape(N_REP, 3, SLOT_MAX, share)
    history_new = (terms[:, 2] + terms[:, 1]) + terms[:, 0]
    history_new = history_new.transpose(1, 0, 2).reshape(SLOT_MAX, TOUCH)
    return (table_rows - update.astype(F32), history_new)


def solution(mesh):
    grid = Mesh(mesh.devices.reshape(8, 8, 8, 2), TBL + REP)
    in_specs = (
        P(REP, TBL),
        P(REP, TBL),
        P(REP, None),
        P(REP, None),
        P(None, TBL),
        P(None, TBL),
        P(TBL, None),
        P(TBL, None),
        P(TBL),
        P(TBL),
        P(),
        P(),
        P(TBL, REP, None),
        P(TBL, None),
        P(TBL, None),
    )
    out_specs = (P(TBL, None), P(TBL, None))
    return jax.shard_map(shards, mesh=grid, in_specs=in_specs, out_specs=out_specs, check_vma=False)
```

```python
import jax
import jax.numpy as jnp
from jax import lax
from jax.experimental import pallas as pl
from jax.experimental.pallas import tpu as pltpu
from jax.sharding import Mesh, PartitionSpec as P

FEATS = 384
EMB = 64
RANK = 512
ROWS = 256
TOUCH = 128
SLOT_MAX = 18
N_TBL = 64
N_REP = 16
PER_DEV = FEATS // N_TBL
SLOT_ROWS = SLOT_MAX // 2
UPDATE_ROWS = SLOT_MAX * 4
SEND_ROWS = UPDATE_ROWS + 8

LEARN_RATE = 0.25
EPSILON = 1e-06

TBL = ("y", "x")
REP = ("z", "core")
BF16 = jnp.bfloat16
F32 = jnp.float32


def exchange(blocks, axis):
    return lax.all_to_all(blocks, axis, split_axis=0, concat_axis=0, tiled=True)


def to_tiles(matrix):
    return matrix.reshape(16, 16, 4, 128).transpose(0, 2, 1, 3).reshape(64, 16, 128)


def from_tiles(tiles):
    return tiles.reshape(16, 4, 16, 128).transpose(0, 2, 1, 3).reshape(ROWS, RANK)


def first_kernel(x_hbm, top_hbm, lift_hbm, squeeze_hbm, out_ref, x_ref, top_ref, lift_ref, squeeze_ref, sems):
    height, core = lax.axis_index("z"), lax.axis_index("core")
    quarter = pl.multiple_of((2 * (height % 2) + core) * 128, 128)
    copies = []
    for source, target, pieces in (
        (x_hbm, x_ref, 2),
        (top_hbm, top_ref, 2),
        (lift_hbm, lift_ref, 4),
        (squeeze_hbm.at[:, pl.ds(quarter, 128)], squeeze_ref, 2),
    ):
        rows = target.shape[0] // pieces
        for i in range(pieces):
            part = pl.ds(i * rows, rows)
            copies.append(pltpu.make_async_copy(source.at[part], target.at[part], sems.at[len(copies)]))
    for copy in copies:
        copy.start()
    row = lax.broadcasted_iota(jnp.int32, (N_TBL * 8, FEATS), 0)
    col = lax.broadcasted_iota(jnp.int32, (N_TBL * 8, FEATS), 1)
    table, column = row & 7, (row >> 4) + 32 * ((height // 2) % 2)
    pick = jnp.where((col == table * EMB + column) & (table < PER_DEV), 1.0, 0.0).astype(BF16)
    for copy in copies:
        copy.wait()
    scaled = (top_ref[...].astype(F32) * x_ref[...].astype(F32)).astype(BF16)
    part = lax.dot_general(scaled, lift_ref[...], (((1,), (1,)), ((), ())), preferred_element_type=F32).astype(BF16)
    for i in range(16):
        for j in range(4):
            out_ref[4 * i + j, :16, :] = part[16 * i : 16 * i + 16, 128 * j : 128 * j + 128]
    moved = jnp.dot(pick, squeeze_ref[...], preferred_element_type=F32)
    out_ref[:, 16:, :] = moved.reshape(N_TBL, 8, 128).astype(BF16)


def first_step(x_zero, grad_top, lift_one, squeeze_zero):
    return pl.pallas_call(
        first_kernel,
        out_shape=jax.ShapeDtypeStruct((N_TBL, 24, 128), BF16),
        in_specs=[pl.BlockSpec(memory_space=pl.ANY)] * 4,
        out_specs=pl.BlockSpec(memory_space=pltpu.VMEM),
        scratch_shapes=[
            pltpu.VMEM(x_zero.shape, BF16),
            pltpu.VMEM(grad_top.shape, BF16),
            pltpu.VMEM(lift_one.shape, BF16),
            pltpu.VMEM((PER_DEV * EMB, 128), BF16),
            pltpu.SemaphoreType.DMA((10,)),
        ],
        compiler_params=pltpu.CompilerParams(vmem_limit_bytes=60 * 2**20),
        name="first_step",
    )(x_zero, grad_top, lift_one, squeeze_zero)


def last_kernel(got_ref, rows_ref, rows_out, history_out, wide):
    wide[...] = got_ref[...].astype(F32).reshape(N_REP * SEND_ROWS, 128)
    for i in range(EMB):
        first = (i // 4) * SEND_ROWS + i % 4
        update = wide[pl.ds(first, SLOT_MAX, stride=4), :]
        rows_out[:, 128 * i : 128 * i + 128] = rows_ref[:, 128 * i : 128 * i + 128] - update
    terms = jnp.concatenate(
        [wide[j * SEND_ROWS + UPDATE_ROWS : (j + 1) * SEND_ROWS, :] for j in range(N_REP)], axis=0
    ).T
    history_out[...] = (terms[64 : 64 + SLOT_MAX] + terms[32 : 32 + SLOT_MAX]) + terms[:SLOT_MAX]


def last_step(got, table_rows):
    vmem = pl.BlockSpec(memory_space=pltpu.VMEM)
    return pl.pallas_call(
        last_kernel,
        out_shape=(
            jax.ShapeDtypeStruct((SLOT_MAX, TOUCH * EMB), F32),
            jax.ShapeDtypeStruct((SLOT_MAX, TOUCH), F32),
        ),
        in_specs=[vmem, vmem],
        out_specs=(vmem, vmem),
        scratch_shapes=[pltpu.VMEM((N_REP * SEND_ROWS, 128), F32)],
        compiler_params=pltpu.CompilerParams(vmem_limit_bytes=24 * 2**20),
        name="last_step",
    )(got, table_rows)


def both(mine, other, bit, axis):
    return jnp.where(bit == 0, jnp.concatenate([mine, other], axis), jnp.concatenate([other, mine], axis))


def shards(
    x_zero,
    grad_top,
    low_zero,
    low_one,
    lift_zero,
    lift_one,
    squeeze_zero,
    squeeze_one,
    bias_zero,
    bias_one,
    table_owner,
    table_slot,
    incidence,
    table_rows,
    row_accum,
):
    rep = lax.axis_index(REP)
    core = lax.axis_index("core")
    height = lax.axis_index("z")
    half, quarter = (height // 2) % 2, rep % 4
    upstream = grad_top.astype(F32)
    embedded = x_zero.astype(F32)

    place = table_owner * SLOT_MAX + table_slot
    wanted = (jnp.arange(N_TBL * SLOT_MAX)[:, None] == place[None, :]).astype(BF16)
    later = 2 * jnp.arange(SLOT_ROWS) + lax.axis_index(TBL) % 2
    second = (jnp.arange(N_TBL)[:, None] * SLOT_MAX + later).reshape(-1)
    padded = jnp.pad(place.reshape(N_TBL, PER_DEV), ((0, 0), (0, 8 - PER_DEV)), constant_values=-1).reshape(-1)
    wanted_second = (second[:, None] == padded[None, :]).astype(BF16)
    incident = lax.optimization_barrier(incidence.astype(BF16))
    gate_one = jnp.dot(low_one, lift_one, preferred_element_type=F32) + bias_one
    gate_zero = jnp.dot(low_zero, lift_zero, preferred_element_type=F32) + bias_zero
    gate_one, gate_zero, wanted, wanted_second = lax.optimization_barrier((gate_one, gate_zero, wanted, wanted_second))

    got = exchange(first_step(x_zero, grad_top, lift_one, squeeze_zero), TBL)
    rank_tile = jnp.sum(got[:, :16].astype(F32), axis=0).astype(BF16)
    part = jnp.dot(wanted_second, got[:, 16:].reshape(N_TBL * 8, 128), preferred_element_type=F32).astype(BF16)
    got = exchange(
        jnp.concatenate(
            [jnp.broadcast_to(rank_tile[None], (N_TBL, 16, 128)), part.reshape(N_TBL, SLOT_ROWS, 128)], axis=1
        ),
        TBL,
    )
    rank_one = from_tiles(got[:, :16])
    part = got[:, 16:]

    grad_mid = upstream + lax.dot_general(
        rank_one, squeeze_one, (((1,), (1,)), ((), ())), preferred_element_type=F32
    )
    part_zero = lax.dot_general(
        (grad_mid * embedded).astype(BF16), lift_zero, (((1,), (1,)), ((), ())), preferred_element_type=F32
    ).astype(BF16)
    pooled_local = (upstream * gate_one + grad_mid * gate_zero + grad_mid).astype(BF16)
    by_column = pooled_local.reshape(2, 128, PER_DEV, EMB).transpose(3, 0, 2, 1).reshape(N_TBL, 2 * PER_DEV, 128)
    send, part = lax.optimization_barrier((jnp.concatenate([to_tiles(part_zero), by_column], axis=1), part))
    got = exchange(send, TBL)
    part = part.reshape(32, 2, SLOT_ROWS, 128).transpose(2, 1, 0, 3).reshape(SLOT_MAX, 32, 128)
    other = lax.ppermute(part, "z", [(i, i ^ 2) for i in range(8)])
    got, part, other = lax.optimization_barrier((got, part, other))
    part = both(part, other, half, 1).reshape(SLOT_MAX * EMB, 128)
    rank_tile = jnp.sum(got[:, :16].astype(F32), axis=0).astype(BF16)

    placed = [
        jnp.dot(
            wanted,
            got[:, 16 + h * PER_DEV : 16 + (h + 1) * PER_DEV].reshape(FEATS, 128),
            preferred_element_type=F32,
        )
        .astype(BF16)
        .reshape(N_TBL, SLOT_MAX, 128)
        for h in range(2)
    ]
    send = jnp.concatenate([jnp.broadcast_to(rank_tile[None], (N_TBL, 16, 128))] + placed, axis=1)
    send, part = lax.optimization_barrier((send, part))
    got = exchange(send, TBL)
    parts = [part] + [lax.ppermute(part, REP, [(i, i ^ k) for i in range(N_REP)]) for k in (1, 2, 3)]
    for bit in (1, 2):
        parts = [jnp.where(quarter & bit == 0, parts[k], parts[k ^ bit]) for k in range(4)]
    squeeze_own = jnp.concatenate(parts, axis=1)
    rank_zero = from_tiles(got[:, :16])
    pooled_slots = (
        got[:, 16:].reshape(EMB, 2, SLOT_MAX, 128).transpose(2, 0, 1, 3).reshape(SLOT_MAX * EMB, ROWS)
    )
    pooled_slots = lax.optimization_barrier(pooled_slots)
    pooled = (
        pooled_slots.astype(F32)
        + lax.dot_general(
            squeeze_own,
            rank_zero,
            (((1,), (1,)), ((), ())),
            preferred_element_type=F32,
        )
    ).astype(BF16)
    partial = jnp.einsum(
        "sbu,seb->sue", incident, pooled.reshape(SLOT_MAX, EMB, ROWS), preferred_element_type=F32
    ).astype(BF16)

    share = TOUCH // N_REP
    got = exchange(partial.reshape(SLOT_MAX, N_REP, 4, 128).transpose(1, 0, 2, 3).reshape(N_REP, SLOT_MAX * 4, 128), REP)
    gradient = jnp.sum(got.astype(F32), axis=0).reshape(SLOT_MAX, 4, 2, EMB)
    history = lax.dynamic_slice(row_accum, (0, rep * share), (SLOT_MAX, share)).reshape(SLOT_MAX, 4, 2)
    history_new = history + jnp.mean(gradient * gradient, axis=3)
    update = LEARN_RATE * gradient / (jnp.sqrt(history_new)[:, :, :, None] + EPSILON)
    update = update.astype(BF16).reshape(SLOT_MAX * 4, 128)
    terms, rest = [], history_new.reshape(SLOT_MAX, share).T
    for _ in range(3):
        term = lax.reduce_precision(rest, 8, 7)
        terms.append(jnp.pad(term, ((0, 0), (0, 32 - SLOT_MAX))))
        rest = rest - term
    terms = jnp.pad(jnp.concatenate(terms, axis=1).astype(BF16), ((0, 0), (0, 32)))
    send = jnp.concatenate([update, terms], axis=0)
    return last_step(exchange(jnp.broadcast_to(send[None], (N_REP,) + send.shape), REP), table_rows)


def solution(mesh):
    grid = Mesh(mesh.devices.reshape(8, 8, 8, 2), TBL + REP)
    in_specs = (
        P(REP, TBL),
        P(REP, TBL),
        P(REP, None),
        P(REP, None),
        P(None, TBL),
        P(None, TBL),
        P(TBL, None),
        P(TBL, None),
        P(TBL),
        P(TBL),
        P(),
        P(),
        P(TBL, REP, None),
        P(TBL, None),
        P(TBL, None),
    )
    out_specs = (P(TBL, None), P(TBL, None))
    return jax.shard_map(shards, mesh=grid, in_specs=in_specs, out_specs=out_specs, check_vma=False)
```

```python
import jax
import jax.numpy as jnp
from jax import lax
from jax.experimental import pallas as pl
from jax.experimental.pallas import tpu as pltpu
from jax.sharding import Mesh, PartitionSpec as P

FEATS = 384
EMB = 64
RANK = 512
ROWS = 256
TOUCH = 128
SLOT_MAX = 18
N_TBL = 64
N_REP = 16
PER_DEV = FEATS // N_TBL
SLOT_ROWS = SLOT_MAX // 2
UPDATE_ROWS = SLOT_MAX * 4
SEND_ROWS = UPDATE_ROWS + 8

LEARN_RATE = 0.25
EPSILON = 1e-06

TBL = ("y", "x")
REP = ("z", "core")
BF16 = jnp.bfloat16
F32 = jnp.float32


def exchange(blocks, axis):
    return lax.all_to_all(blocks, axis, split_axis=0, concat_axis=0, tiled=True)


def exchange_rows(parts, axis):
    blocks, rows = parts[0].shape[0], sum(part.shape[1] for part in parts)
    spare = -rows % 4
    if spare:
        parts = parts + [jnp.zeros((blocks, spare, 128), BF16)]
    sent = jnp.concatenate(parts, axis=1).reshape(blocks, (rows + spare) // 4, 4, 128)
    return sent, lambda sent: exchange(sent, axis).reshape(blocks, rows + spare, 128)[:, :rows]


def to_tiles(matrix):
    return matrix.reshape(16, 16, 4, 128).transpose(0, 2, 1, 3).reshape(64, 16, 128)


def from_tiles(tiles):
    return tiles.reshape(16, 4, 16, 128).transpose(0, 2, 1, 3).reshape(ROWS, RANK)


def first_kernel(x_hbm, top_hbm, lift_hbm, squeeze_hbm, out_ref, x_ref, top_ref, lift_ref, squeeze_ref, sems):
    height, core = lax.axis_index("z"), lax.axis_index("core")
    quarter = pl.multiple_of((2 * (height % 2) + core) * 128, 128)
    copies = []
    for source, target, pieces in (
        (x_hbm, x_ref, 2),
        (top_hbm, top_ref, 2),
        (lift_hbm, lift_ref, 4),
        (squeeze_hbm.at[:, pl.ds(quarter, 128)], squeeze_ref, 2),
    ):
        rows = target.shape[0] // pieces
        for i in range(pieces):
            part = pl.ds(i * rows, rows)
            copies.append(pltpu.make_async_copy(source.at[part], target.at[part], sems.at[len(copies)]))
    for copy in copies:
        copy.start()
    row = lax.broadcasted_iota(jnp.int32, (N_TBL * 8, FEATS), 0)
    col = lax.broadcasted_iota(jnp.int32, (N_TBL * 8, FEATS), 1)
    table, column = row & 7, (row >> 4) + 32 * ((height // 2) % 2)
    pick = jnp.where((col == table * EMB + column) & (table < PER_DEV), 1.0, 0.0).astype(BF16)
    for copy in copies:
        copy.wait()
    scaled = (top_ref[...].astype(F32) * x_ref[...].astype(F32)).astype(BF16)
    part = lax.dot_general(scaled, lift_ref[...], (((1,), (1,)), ((), ())), preferred_element_type=F32).astype(BF16)
    for i in range(16):
        for j in range(4):
            out_ref[4 * i + j, :16, :] = part[16 * i : 16 * i + 16, 128 * j : 128 * j + 128]
    moved = jnp.dot(pick, squeeze_ref[...], preferred_element_type=F32)
    out_ref[:, 16:, :] = moved.reshape(N_TBL, 8, 128).astype(BF16)


def first_step(x_zero, grad_top, lift_one, squeeze_zero):
    return pl.pallas_call(
        first_kernel,
        out_shape=jax.ShapeDtypeStruct((N_TBL, 24, 128), BF16),
        in_specs=[pl.BlockSpec(memory_space=pl.ANY)] * 4,
        out_specs=pl.BlockSpec(memory_space=pltpu.VMEM),
        scratch_shapes=[
            pltpu.VMEM(x_zero.shape, BF16),
            pltpu.VMEM(grad_top.shape, BF16),
            pltpu.VMEM(lift_one.shape, BF16),
            pltpu.VMEM((PER_DEV * EMB, 128), BF16),
            pltpu.SemaphoreType.DMA((10,)),
        ],
        compiler_params=pltpu.CompilerParams(vmem_limit_bytes=60 * 2**20),
        name="first_step",
    )(x_zero, grad_top, lift_one, squeeze_zero)


def last_kernel(got_ref, rows_ref, rows_out, history_out, wide):
    wide[...] = got_ref[...].astype(F32).reshape(N_REP * SEND_ROWS, 128)
    for i in range(EMB):
        first = (i // 4) * SEND_ROWS + i % 4
        update = wide[pl.ds(first, SLOT_MAX, stride=4), :]
        rows_out[:, 128 * i : 128 * i + 128] = rows_ref[:, 128 * i : 128 * i + 128] - update
    terms = jnp.concatenate(
        [wide[j * SEND_ROWS + UPDATE_ROWS : (j + 1) * SEND_ROWS, :] for j in range(N_REP)], axis=0
    ).T
    history_out[...] = (terms[64 : 64 + SLOT_MAX] + terms[32 : 32 + SLOT_MAX]) + terms[:SLOT_MAX]


def last_step(got, table_rows):
    vmem = pl.BlockSpec(memory_space=pltpu.VMEM)
    return pl.pallas_call(
        last_kernel,
        out_shape=(
            jax.ShapeDtypeStruct((SLOT_MAX, TOUCH * EMB), F32),
            jax.ShapeDtypeStruct((SLOT_MAX, TOUCH), F32),
        ),
        in_specs=[vmem, vmem],
        out_specs=(vmem, vmem),
        scratch_shapes=[pltpu.VMEM((N_REP * SEND_ROWS, 128), F32)],
        compiler_params=pltpu.CompilerParams(vmem_limit_bytes=24 * 2**20),
        name="last_step",
    )(got, table_rows)


def both(mine, other, bit, axis):
    return jnp.where(bit == 0, jnp.concatenate([mine, other], axis), jnp.concatenate([other, mine], axis))


def shards(
    x_zero,
    grad_top,
    low_zero,
    low_one,
    lift_zero,
    lift_one,
    squeeze_zero,
    squeeze_one,
    bias_zero,
    bias_one,
    table_owner,
    table_slot,
    incidence,
    table_rows,
    row_accum,
):
    rep = lax.axis_index(REP)
    core = lax.axis_index("core")
    height = lax.axis_index("z")
    half, quarter = (height // 2) % 2, rep % 4
    upstream = grad_top.astype(F32)
    embedded = x_zero.astype(F32)

    place = table_owner * SLOT_MAX + table_slot
    wanted = (jnp.arange(N_TBL * SLOT_MAX)[:, None] == place[None, :]).astype(BF16)
    later = 2 * jnp.arange(SLOT_ROWS) + lax.axis_index(TBL) % 2
    second = (jnp.arange(N_TBL)[:, None] * SLOT_MAX + later).reshape(-1)
    padded = jnp.pad(place.reshape(N_TBL, PER_DEV), ((0, 0), (0, 8 - PER_DEV)), constant_values=-1).reshape(-1)
    wanted_second = (second[:, None] == padded[None, :]).astype(BF16)
    incident = lax.optimization_barrier(incidence.astype(BF16))
    gate_one = jnp.dot(low_one, lift_one, preferred_element_type=F32) + bias_one
    gate_zero = jnp.dot(low_zero, lift_zero, preferred_element_type=F32) + bias_zero
    gate_one, gate_zero, wanted, wanted_second = lax.optimization_barrier((gate_one, gate_zero, wanted, wanted_second))

    got = exchange(first_step(x_zero, grad_top, lift_one, squeeze_zero), TBL)
    rank_tile = jnp.sum(got[:, :16].astype(F32), axis=0).astype(BF16)
    part = jnp.dot(wanted_second, got[:, 16:].reshape(N_TBL * 8, 128), preferred_element_type=F32).astype(BF16)
    send, move = exchange_rows(
        [jnp.broadcast_to(rank_tile[None], (N_TBL, 16, 128)), part.reshape(N_TBL, SLOT_ROWS, 128)], TBL
    )
    got = move(send)
    rank_one = from_tiles(got[:, :16])
    part = got[:, 16:]

    grad_mid = upstream + lax.dot_general(
        rank_one, squeeze_one, (((1,), (1,)), ((), ())), preferred_element_type=F32
    )
    part_zero = lax.dot_general(
        (grad_mid * embedded).astype(BF16), lift_zero, (((1,), (1,)), ((), ())), preferred_element_type=F32
    ).astype(BF16)
    pooled_local = (upstream * gate_one + grad_mid * gate_zero + grad_mid).astype(BF16)
    by_column = pooled_local.reshape(2, 128, PER_DEV, EMB).transpose(3, 0, 2, 1).reshape(N_TBL, 2 * PER_DEV, 128)
    send, move = exchange_rows([to_tiles(part_zero), by_column], TBL)
    send, part = lax.optimization_barrier((send, part))
    got = move(send)
    part = part.reshape(32, 2, SLOT_ROWS, 128).transpose(2, 1, 0, 3).reshape(SLOT_MAX, 32, 128)
    other = lax.ppermute(part, "z", [(i, i ^ 2) for i in range(8)])
    got, part, other = lax.optimization_barrier((got, part, other))
    part = both(part, other, half, 1).reshape(SLOT_MAX * EMB, 128)
    rank_tile = jnp.sum(got[:, :16].astype(F32), axis=0).astype(BF16)

    placed = [
        jnp.dot(
            wanted,
            got[:, 16 + h * PER_DEV : 16 + (h + 1) * PER_DEV].reshape(FEATS, 128),
            preferred_element_type=F32,
        )
        .astype(BF16)
        .reshape(N_TBL, SLOT_MAX, 128)
        for h in range(2)
    ]
    send, move = exchange_rows([jnp.broadcast_to(rank_tile[None], (N_TBL, 16, 128))] + placed, TBL)
    send, part = lax.optimization_barrier((send, part))
    got = move(send)
    parts = [part] + [lax.ppermute(part, REP, [(i, i ^ k) for i in range(N_REP)]) for k in (1, 2, 3)]
    squeeze_own = jnp.concatenate(parts, axis=1)
    tiles = got[:, :16].reshape(16, 4, 16, 128)
    blocks = [tiles[:, k] for k in range(4)]
    for bit in (1, 2):
        blocks = [jnp.where(quarter & bit == 0, blocks[k], blocks[k ^ bit]) for k in range(4)]
    rank_zero = jnp.concatenate([block.reshape(ROWS, 128) for block in blocks], axis=1)
    pooled_slots = (
        got[:, 16:].reshape(EMB, 2, SLOT_MAX, 128).transpose(2, 0, 1, 3).reshape(SLOT_MAX * EMB, ROWS)
    )
    pooled_slots = lax.optimization_barrier(pooled_slots)
    pooled = (
        pooled_slots.astype(F32)
        + lax.dot_general(
            squeeze_own,
            rank_zero,
            (((1,), (1,)), ((), ())),
            preferred_element_type=F32,
        )
    ).astype(BF16)
    partial = jnp.einsum(
        "sbu,seb->sue", incident, pooled.reshape(SLOT_MAX, EMB, ROWS), preferred_element_type=F32
    ).astype(BF16)

    share = TOUCH // N_REP
    got = exchange(partial.reshape(SLOT_MAX, N_REP, 4, 128).transpose(1, 0, 2, 3).reshape(N_REP, SLOT_MAX * 4, 128), REP)
    gradient = jnp.sum(got.astype(F32), axis=0).reshape(SLOT_MAX, 4, 2, EMB)
    history = lax.dynamic_slice(row_accum, (0, rep * share), (SLOT_MAX, share)).reshape(SLOT_MAX, 4, 2)
    history_new = history + jnp.mean(gradient * gradient, axis=3)
    update = LEARN_RATE * gradient / (jnp.sqrt(history_new)[:, :, :, None] + EPSILON)
    update = update.astype(BF16).reshape(SLOT_MAX * 4, 128)
    terms, rest = [], history_new.reshape(SLOT_MAX, share).T
    for _ in range(3):
        term = lax.reduce_precision(rest, 8, 7)
        terms.append(jnp.pad(term, ((0, 0), (0, 32 - SLOT_MAX))))
        rest = rest - term
    terms = jnp.pad(jnp.concatenate(terms, axis=1).astype(BF16), ((0, 0), (0, 32)))
    send = jnp.concatenate([update, terms], axis=0)
    return last_step(exchange(jnp.broadcast_to(send[None], (N_REP,) + send.shape), REP), table_rows)


def solution(mesh):
    grid = Mesh(mesh.devices.reshape(8, 8, 8, 2), TBL + REP)
    in_specs = (
        P(REP, TBL),
        P(REP, TBL),
        P(REP, None),
        P(REP, None),
        P(None, TBL),
        P(None, TBL),
        P(TBL, None),
        P(TBL, None),
        P(TBL),
        P(TBL),
        P(),
        P(),
        P(TBL, REP, None),
        P(TBL, None),
        P(TBL, None),
    )
    out_specs = (P(TBL, None), P(TBL, None))
    return jax.shard_map(shards, mesh=grid, in_specs=in_specs, out_specs=out_specs, check_vma=False)
```

```python
import jax
import jax.numpy as jnp
from jax import lax
from jax.experimental import pallas as pl
from jax.experimental.pallas import tpu as pltpu
from jax.sharding import Mesh, PartitionSpec as P

FEATS = 384
EMB = 64
RANK = 512
ROWS = 256
TOUCH = 128
SLOT_MAX = 18
N_TBL = 64
N_REP = 16
PER_DEV = FEATS // N_TBL
SLOT_ROWS = SLOT_MAX // 2
UPDATE_ROWS = SLOT_MAX * 4
SEND_ROWS = UPDATE_ROWS + 8

LEARN_RATE = 0.25
EPSILON = 1e-06

TBL = ("y", "x")
REP = ("z", "core")
BF16 = jnp.bfloat16
F32 = jnp.float32


def exchange(blocks, axis):
    return lax.all_to_all(blocks, axis, split_axis=0, concat_axis=0, tiled=True)


def exchange_rows(parts, axis):
    blocks, rows = parts[0].shape[0], sum(part.shape[1] for part in parts)
    spare = -rows % 4
    if spare:
        parts = parts + [jnp.zeros((blocks, spare, 128), BF16)]
    sent = jnp.concatenate(parts, axis=1).reshape(blocks, (rows + spare) // 4, 4, 128)
    return sent, lambda sent: exchange(sent, axis).reshape(blocks, rows + spare, 128)[:, :rows]


def to_tiles(matrix):
    return matrix.reshape(16, 16, 4, 128).transpose(0, 2, 1, 3).reshape(64, 16, 128)


def from_tiles(tiles):
    return tiles.reshape(16, 4, 16, 128).transpose(0, 2, 1, 3).reshape(ROWS, RANK)


def first_kernel(x_hbm, top_hbm, lift_hbm, squeeze_hbm, out_ref, x_ref, top_ref, lift_ref, squeeze_ref, sems):
    height, core = lax.axis_index("z"), lax.axis_index("core")
    quarter = pl.multiple_of((2 * (height % 2) + core) * 128, 128)
    copies = []
    for source, target, pieces in (
        (x_hbm, x_ref, 2),
        (top_hbm, top_ref, 2),
        (lift_hbm, lift_ref, 4),
        (squeeze_hbm.at[:, pl.ds(quarter, 128)], squeeze_ref, 2),
    ):
        rows = target.shape[0] // pieces
        for i in range(pieces):
            part = pl.ds(i * rows, rows)
            copies.append(pltpu.make_async_copy(source.at[part], target.at[part], sems.at[len(copies)]))
    for copy in copies:
        copy.start()
    row = lax.broadcasted_iota(jnp.int32, (N_TBL * 8, FEATS), 0)
    col = lax.broadcasted_iota(jnp.int32, (N_TBL * 8, FEATS), 1)
    table, column = row & 7, (row >> 4) + 32 * ((height // 2) % 2)
    pick = jnp.where((col == table * EMB + column) & (table < PER_DEV), 1.0, 0.0).astype(BF16)
    for copy in copies:
        copy.wait()
    scaled = (top_ref[...].astype(F32) * x_ref[...].astype(F32)).astype(BF16)
    part = lax.dot_general(scaled, lift_ref[...], (((1,), (1,)), ((), ())), preferred_element_type=F32).astype(BF16)
    for i in range(16):
        for j in range(4):
            out_ref[4 * i + j, :16, :] = part[16 * i : 16 * i + 16, 128 * j : 128 * j + 128]
    moved = jnp.dot(pick, squeeze_ref[...], preferred_element_type=F32)
    out_ref[:, 16:, :] = moved.reshape(N_TBL, 8, 128).astype(BF16)


def first_step(x_zero, grad_top, lift_one, squeeze_zero):
    return pl.pallas_call(
        first_kernel,
        out_shape=jax.ShapeDtypeStruct((N_TBL, 24, 128), BF16),
        in_specs=[pl.BlockSpec(memory_space=pl.ANY)] * 4,
        out_specs=pl.BlockSpec(memory_space=pltpu.VMEM),
        scratch_shapes=[
            pltpu.VMEM(x_zero.shape, BF16),
            pltpu.VMEM(grad_top.shape, BF16),
            pltpu.VMEM(lift_one.shape, BF16),
            pltpu.VMEM((PER_DEV * EMB, 128), BF16),
            pltpu.SemaphoreType.DMA((10,)),
        ],
        compiler_params=pltpu.CompilerParams(vmem_limit_bytes=60 * 2**20),
        name="first_step",
    )(x_zero, grad_top, lift_one, squeeze_zero)


def last_kernel(got_ref, rows_ref, rows_out, history_out, wide):
    wide[...] = got_ref[...].astype(F32).reshape(N_REP * SEND_ROWS, 128)
    for i in range(EMB):
        first = (i // 4) * SEND_ROWS + i % 4
        update = wide[pl.ds(first, SLOT_MAX, stride=4), :]
        rows_out[:, 128 * i : 128 * i + 128] = rows_ref[:, 128 * i : 128 * i + 128] - update
    terms = jnp.concatenate(
        [wide[j * SEND_ROWS + UPDATE_ROWS : (j + 1) * SEND_ROWS, :] for j in range(N_REP)], axis=0
    ).T
    history_out[...] = (terms[64 : 64 + SLOT_MAX] + terms[32 : 32 + SLOT_MAX]) + terms[:SLOT_MAX]


def last_step(got, table_rows):
    vmem = pl.BlockSpec(memory_space=pltpu.VMEM)
    return pl.pallas_call(
        last_kernel,
        out_shape=(
            jax.ShapeDtypeStruct((SLOT_MAX, TOUCH * EMB), F32),
            jax.ShapeDtypeStruct((SLOT_MAX, TOUCH), F32),
        ),
        in_specs=[vmem, vmem],
        out_specs=(vmem, vmem),
        scratch_shapes=[pltpu.VMEM((N_REP * SEND_ROWS, 128), F32)],
        compiler_params=pltpu.CompilerParams(vmem_limit_bytes=24 * 2**20),
        name="last_step",
    )(got, table_rows)


def both(mine, other, bit, axis):
    return jnp.where(bit == 0, jnp.concatenate([mine, other], axis), jnp.concatenate([other, mine], axis))


def shards(
    x_zero,
    grad_top,
    low_zero,
    low_one,
    lift_zero,
    lift_one,
    squeeze_zero,
    squeeze_one,
    bias_zero,
    bias_one,
    table_owner,
    table_slot,
    incidence,
    table_rows,
    row_accum,
):
    rep = lax.axis_index(REP)
    core = lax.axis_index("core")
    height = lax.axis_index("z")
    half, quarter = (height // 2) % 2, rep % 4
    upstream = grad_top.astype(F32)
    embedded = x_zero.astype(F32)

    place = table_owner * SLOT_MAX + table_slot
    wanted = (jnp.arange(N_TBL * SLOT_MAX)[:, None] == place[None, :]).astype(BF16)
    later = 2 * jnp.arange(SLOT_ROWS) + lax.axis_index(TBL) % 2
    second = (jnp.arange(N_TBL)[:, None] * SLOT_MAX + later).reshape(-1)
    padded = jnp.pad(place.reshape(N_TBL, PER_DEV), ((0, 0), (0, 8 - PER_DEV)), constant_values=-1).reshape(-1)
    wanted_second = (second[:, None] == padded[None, :]).astype(BF16)
    incident = lax.optimization_barrier(incidence.astype(BF16))
    gate_one = jnp.dot(low_one, lift_one, preferred_element_type=F32) + bias_one
    gate_zero = jnp.dot(low_zero, lift_zero, preferred_element_type=F32) + bias_zero
    gate_one, gate_zero, wanted, wanted_second = lax.optimization_barrier((gate_one, gate_zero, wanted, wanted_second))

    got = exchange(first_step(x_zero, grad_top, lift_one, squeeze_zero), TBL)
    rank_tile = jnp.sum(got[:, :16].astype(F32), axis=0).astype(BF16)
    part = jnp.dot(wanted_second, got[:, 16:].reshape(N_TBL * 8, 128), preferred_element_type=F32).astype(BF16)
    send, move = exchange_rows(
        [jnp.broadcast_to(rank_tile[None], (N_TBL, 16, 128)), part.reshape(N_TBL, SLOT_ROWS, 128)], TBL
    )
    got = move(send)
    rank_one = from_tiles(got[:, :16])
    part = got[:, 16:]

    grad_mid = upstream + lax.dot_general(
        rank_one, squeeze_one, (((1,), (1,)), ((), ())), preferred_element_type=F32
    )
    part_zero = lax.dot_general(
        (grad_mid * embedded).astype(BF16), lift_zero, (((1,), (1,)), ((), ())), preferred_element_type=F32
    ).astype(BF16)
    pooled_local = (upstream * gate_one + grad_mid * gate_zero + grad_mid).astype(BF16)
    by_column = pooled_local.reshape(2, 128, PER_DEV, EMB).transpose(3, 0, 2, 1).reshape(N_TBL, 2 * PER_DEV, 128)
    send, move = exchange_rows([to_tiles(part_zero), by_column], TBL)
    send, part = lax.optimization_barrier((send, part))
    got = move(send)
    part = part.reshape(32, 2, SLOT_ROWS, 128).transpose(2, 1, 0, 3).reshape(SLOT_MAX, 32, 128)
    other = lax.ppermute(part, "z", [(i, i ^ 2) for i in range(8)])
    got, part, other = lax.optimization_barrier((got, part, other))
    part = both(part, other, half, 1).reshape(SLOT_MAX * EMB, 128)
    rank_tile = jnp.sum(got[:, :16].astype(F32), axis=0).astype(BF16)

    placed = [
        jnp.dot(
            wanted,
            got[:, 16 + h * PER_DEV : 16 + (h + 1) * PER_DEV].reshape(FEATS, 128),
            preferred_element_type=F32,
        )
        .astype(BF16)
        .reshape(N_TBL, SLOT_MAX, 128)
        for h in range(2)
    ]
    send, move = exchange_rows([jnp.broadcast_to(rank_tile[None], (N_TBL, 16, 128))] + placed, TBL)
    send, part = lax.optimization_barrier((send, part))
    got = move(send)
    parts = [part] + [lax.ppermute(part, REP, [(i, i ^ k) for i in range(N_REP)]) for k in (1, 2, 3)]
    for bit in (1, 2):
        parts = [jnp.where(quarter & bit == 0, parts[k], parts[k ^ bit]) for k in range(4)]
    squeeze_own = jnp.concatenate(parts, axis=1)
    rank_zero = from_tiles(got[:, :16])
    pooled_slots = (
        got[:, 16:].reshape(EMB, 2, SLOT_MAX, 128).transpose(2, 0, 1, 3).reshape(SLOT_MAX * EMB, ROWS)
    )
    pooled_slots = lax.optimization_barrier(pooled_slots)
    pooled = (
        pooled_slots.astype(F32)
        + lax.dot_general(
            squeeze_own,
            rank_zero,
            (((1,), (1,)), ((), ())),
            preferred_element_type=F32,
        )
    ).astype(BF16)
    partial = jnp.einsum(
        "sbu,seb->sue", incident, pooled.reshape(SLOT_MAX, EMB, ROWS), preferred_element_type=F32
    ).astype(BF16)

    share = TOUCH // N_REP
    got = exchange(partial.reshape(SLOT_MAX, N_REP, 4, 128).transpose(1, 0, 2, 3).reshape(N_REP, SLOT_MAX * 4, 128), REP)
    gradient = jnp.sum(got.astype(F32), axis=0).reshape(SLOT_MAX, 4, 2, EMB)
    history = lax.dynamic_slice(row_accum, (0, rep * share), (SLOT_MAX, share)).reshape(SLOT_MAX, 4, 2)
    history_new = history + jnp.mean(gradient * gradient, axis=3)
    update = LEARN_RATE * gradient / (jnp.sqrt(history_new)[:, :, :, None] + EPSILON)
    update = update.astype(BF16).reshape(SLOT_MAX * 4, 128)
    terms, rest = [], history_new.reshape(SLOT_MAX, share).T
    for _ in range(3):
        term = lax.reduce_precision(rest, 8, 7)
        terms.append(jnp.pad(term, ((0, 0), (0, 32 - SLOT_MAX))))
        rest = rest - term
    terms = jnp.pad(jnp.concatenate(terms, axis=1).astype(BF16), ((0, 0), (0, 32)))
    send = jnp.concatenate([update, terms], axis=0)
    return last_step(exchange(jnp.broadcast_to(send[None], (N_REP,) + send.shape), REP), table_rows)


def solution(mesh):
    grid = Mesh(mesh.devices.reshape(8, 8, 8, 2), TBL + REP)
    in_specs = (
        P(REP, TBL),
        P(REP, TBL),
        P(REP, None),
        P(REP, None),
        P(None, TBL),
        P(None, TBL),
        P(TBL, None),
        P(TBL, None),
        P(TBL),
        P(TBL),
        P(),
        P(),
        P(TBL, REP, None),
        P(TBL, None),
        P(TBL, None),
    )
    out_specs = (P(TBL, None), P(TBL, None))
    return jax.shard_map(shards, mesh=grid, in_specs=in_specs, out_specs=out_specs, check_vma=False)
```
